512 devices in a mesh: proto: 64 (over z, y), batch: 8 (over x, core).
Axes of the slice: x: 4, y: 8, z: 8, core: 2. Of those that a mesh axis runs over, the one named last changes fastest.
Arguments:
- teacher_feats: bfloat16 [512, 4096], P('batch', 'proto'), may hold values from -8 to 8
- teacher_protos: bfloat16 [4096, 131072], P(None, ('proto', 'batch')), may hold values from -1 to 1
- student_feats: bfloat16 [2048, 1024], P('batch'), may hold values from -24 to 24
- crop_table: bfloat16 [4, 1024], replicated, may hold values from -6 to 6
- student_protos: bfloat16 [1024, 131072], P('batch', 'proto'), may hold values from -2 to 2
- assign: int32 [2048], P('batch'), may hold values from 0 to 63
- crop_ids: int32 [2048], P('batch'), may hold values from 0 to 3
Outputs:
- feat_grad: bfloat16 [2048, 1024], P('batch')
- weight_grad: bfloat16 [1024, 131072], P('batch', 'proto')
The draws below stay inside these ranges and needn't reach their ends.
All inputs are finite; a program needn't handle non-finite values.
Results may differ from the reference program's by a relative error of at most 0.015.
Values may be sent and summed in bfloat16 or wider, within the bound.
No kernel may reach another device: no remote copies, remote signals or barrier semaphores. Data moves between devices by JAX's collectives and lax.ppermute only.
A program may use at most 64 MiB of HBM per device.

```python
import jax
import jax.numpy as jnp
from jax import lax

D = 4096
DS = 1024
IMG_DEV = 64
NS_DEV = 256
ITERS = 3
NCROP = 4
IMAGES = 512
PROTOS = 131072
NS = 2048
N_BATCH = 8


def column_draw(column_key, height):
    values = jax.random.normal(column_key, (height,), jnp.float32)
    return jnp.clip(values, -6.0, 6.0) / jnp.sqrt(jnp.float32(height))


def proto_columns(source_key, columns, height):

    def single(position):
        return column_draw(jax.random.fold_in(source_key, position), height)
    return jax.vmap(single)(columns)


def teacher_columns(source_key, columns):
    values = proto_columns(jax.random.fold_in(source_key, 11), columns, D)
    keep = (jnp.arange(D, dtype=jnp.int32) >= 4).astype(jnp.float32)
    return values * keep[None, :]


def student_columns(source_key, columns):
    return proto_columns(jax.random.fold_in(source_key, 13), columns, DS)


def member_flags(flag_key, count, members):
    order = jax.random.permutation(flag_key, count)
    return (order < members).astype(jnp.float32)


def group_coords(group_key, count, lead_count, lead_value, other_value):
    lead = member_flags(jax.random.fold_in(group_key, 0), count, lead_count)
    first = lead_value * (2.0 * lead - 1.0)
    others = [other_value * member_flags(jax.random.fold_in(group_key, j), count, count // 2) for j in range(1, 4)]
    return jnp.stack([first] + others, axis=1)


def draw_teacher_protos(key, part):
    columns = teacher_columns(key, jnp.arange(PROTOS, dtype=jnp.int32))
    coords = group_coords(jax.random.fold_in(key, 17), PROTOS, PROTOS // 8, 0.5, 0.5)
    columns = columns.at[:, 0:4].set(coords)
    return columns.T.astype(jnp.bfloat16)


def draw_teacher_feats(key, part):
    key = jax.random.fold_in(key, 21)
    coords = group_coords(jax.random.fold_in(key, 5), IMAGES, IMAGES // 2, 3.0, 1.54)
    feats = jnp.clip(jax.random.normal(key, (IMAGES, D), jnp.float32), -6.0, 6.0)
    feats = feats.at[:, 0:4].set(coords)
    return feats.astype(jnp.bfloat16)


def draw_student_protos(key, part):
    columns = student_columns(key, jnp.arange(PROTOS, dtype=jnp.int32))
    return columns.T.astype(jnp.bfloat16)


def draw_student_feats(key, part):
    key = jax.random.fold_in(key, 41)
    feats = jnp.clip(jax.random.normal(key, (NS, DS), jnp.float32), -6.0, 6.0)
    return feats.astype(jnp.bfloat16)


def place_ends(entries, own_key, low, top_value):
    longest = entries.shape.index(max(entries.shape))
    spots = []
    for shift in (0, 1):
        where = [jax.random.randint(jax.random.fold_in(own_key, axis), (), 0, length) for axis, length in enumerate(entries.shape)]
        where[longest] = (where[longest] + shift) % entries.shape[longest]
        spots.append(tuple(where))
    return entries.at[spots[0]].set(low).at[spots[1]].set(top_value)


def normal_values(own_key, shape, scale, most, held_as=jnp.bfloat16):
    return jnp.clip(scale * jax.random.normal(own_key, shape, jnp.float32), -most, most).astype(held_as)


def setup_inputs(seed: int = 0) -> dict:
    arg_keys = jax.random.split(jax.random.key(seed), 8)
    teacher_feats = draw_teacher_feats(jax.random.fold_in(arg_keys[7], 71), 0)
    teacher_protos = draw_teacher_protos(jax.random.fold_in(arg_keys[7], 71), 0)
    student_feats = draw_student_feats(jax.random.fold_in(arg_keys[7], 71), 0)
    crop_table = normal_values(arg_keys[3], (NCROP, DS), 1.0, 6.0)
    student_protos = draw_student_protos(jax.random.fold_in(arg_keys[7], 71), 0)
    assign = place_ends(jax.random.randint(arg_keys[5], (NS,), 0, IMG_DEV), jax.random.fold_in(arg_keys[5], 1), 0, IMG_DEV - 1).astype(jnp.int32)
    crop_ids = place_ends(jax.random.randint(arg_keys[6], (NS,), 0, NCROP), jax.random.fold_in(arg_keys[6], 1), 0, NCROP - 1).astype(jnp.int32)
    return {"teacher_feats": teacher_feats, "teacher_protos": teacher_protos, "student_feats": student_feats, "crop_table": crop_table, "student_protos": student_protos, "assign": assign, "crop_ids": crop_ids}


teacher_scale = 3.0
student_scale = 2.0


def reference(teacher_feats, teacher_protos, student_feats, crop_table, student_protos, assign, crop_ids):
    products = jnp.dot(teacher_feats, teacher_protos, preferred_element_type=jnp.float32)
    logits = teacher_scale * products
    weights = jnp.exp(logits - jnp.max(logits, axis=0, keepdims=True))
    for sweep in range(ITERS):
        weights = weights / jnp.sum(weights, axis=0, keepdims=True)
        weights = weights / jnp.sum(weights, axis=1, keepdims=True)
    targets = weights.astype(jnp.bfloat16)
    chosen = (crop_ids[:, None] == jnp.arange(NCROP, dtype=jnp.int32)[None, :]).astype(jnp.bfloat16)
    table_rows = jnp.dot(chosen, crop_table, preferred_element_type=jnp.float32)
    hidden = (student_feats.astype(jnp.float32) + table_rows).astype(jnp.bfloat16)
    image_ids = (assign + (jnp.arange(NS, dtype=jnp.int32) // NS_DEV) * IMG_DEV).astype(jnp.int32)
    hidden_blocks = hidden.reshape(N_BATCH, NS_DEV, DS)
    image_blocks = image_ids.reshape(N_BATCH, NS_DEV)

    def one_block(running, inputs):
        block_hidden, block_ids = inputs
        crop_targets = jnp.take(targets, block_ids, axis=0).astype(jnp.float32)
        scores = student_scale * jnp.dot(block_hidden, student_protos, preferred_element_type=jnp.float32)
        maximum = jnp.max(scores, axis=1, keepdims=True)
        expsum = jnp.sum(jnp.exp(scores - maximum), axis=1, keepdims=True)
        probabilities = jnp.exp(scores - maximum) / expsum
        logit_grad = (student_scale * (probabilities - crop_targets)).astype(jnp.bfloat16)
        feat_block = lax.dot_general(logit_grad, student_protos, (((1,), (1,)), ((), ())),
                                     preferred_element_type=jnp.float32).astype(jnp.bfloat16)
        weight_part = lax.dot_general(block_hidden, logit_grad, (((0,), (0,)), ((), ())),
                                      preferred_element_type=jnp.float32).astype(jnp.bfloat16)
        weight_part = lax.optimization_barrier(weight_part)
        return running + weight_part.astype(jnp.float32), feat_block

    start_sum = jnp.zeros((DS, PROTOS), jnp.float32)
    weight_sum, feat_blocks = lax.scan(one_block, start_sum, (hidden_blocks, image_blocks))
    feat_grad = feat_blocks.reshape(NS, DS)
    return feat_grad, weight_sum.astype(jnp.bfloat16)
```

```python
import jax
import jax.numpy as jnp
from jax import lax
from jax.sharding import Mesh, PartitionSpec as P

ITERS = 3

teacher_scale = 3.0
student_scale = 2.0

BATCH = ("x", "core")
PROTO = ("z", "y")


def spread(block, axes):
    count = lax.axis_size(axes)
    return lax.all_to_all(
        jnp.broadcast_to(block[None], (count,) + block.shape),
        axes,
        split_axis=0,
        concat_axis=0,
        tiled=True,
    )


def exchange(parts, axes):
    return lax.all_to_all(parts, axes, split_axis=0, concat_axis=0, tiled=True)


def total_over_all(partial):
    near = jnp.sum(spread(partial, BATCH), axis=0)
    return jnp.sum(spread(near, PROTO), axis=0)


def dot0(left, right):
    return lax.dot_general(
        left, right, (((0,), (0,)), ((), ())), preferred_element_type=jnp.float32
    )


def dot1(left, right):
    return lax.dot_general(
        left, right, (((1,), (1,)), ((), ())), preferred_element_type=jnp.float32
    )


def on_device(
    teacher_feats, teacher_protos, student_feats, crop_table, student_protos, assign, crop_ids
):
    core = lax.axis_index("core")
    x_pos = lax.axis_index("x")
    n_x, n_proto, n_batch = lax.axis_size("x"), lax.axis_size(PROTO), lax.axis_size(BATCH)
    images, features = teacher_feats.shape
    crops, width = student_feats.shape
    half = n_x * images

    near = spread(teacher_feats, "x").reshape(half, features).T
    near = spread(near, "y").reshape(-1, half)
    own_feats = lax.all_gather(near, "z", axis=0, tiled=True)
    other_feats = lax.ppermute(own_feats, "core", [(0, 1), (1, 0)])
    own = dot0(own_feats, teacher_protos)
    other = dot0(other_feats, teacher_protos)
    first = core == 0
    products = jnp.concatenate(
        [jnp.where(first, own, other), jnp.where(first, other, own)], axis=0
    )

    chosen = (
        crop_ids[:, None] == jnp.arange(crop_table.shape[0], dtype=jnp.int32)[None, :]
    ).astype(jnp.bfloat16)
    table_rows = jnp.dot(chosen, crop_table, preferred_element_type=jnp.float32)
    hidden = (student_feats.astype(jnp.float32) + table_rows).astype(jnp.bfloat16)
    picks = (
        assign[:, None] == jnp.arange(images, dtype=jnp.int32)[None, :]
    ).astype(jnp.bfloat16)
    image_hidden = dot0(picks, hidden).astype(jnp.bfloat16)
    full_protos = lax.all_gather(student_protos, BATCH, axis=0, tiled=True)
    scores = student_scale * jnp.dot(hidden, full_protos, preferred_element_type=jnp.float32)
    peak = jnp.max(scores, axis=1)
    powers = jnp.exp(scores - peak[:, None])
    both = spread(jnp.stack([peak, jnp.sum(powers, axis=1)]), PROTO)
    top = jnp.max(both[:, 0], axis=0)
    denominator = jnp.sum(both[:, 1] * jnp.exp(both[:, 0] - top[None]), axis=0)
    factor = student_scale * jnp.exp(peak - top) / denominator
    soft = (powers * factor[:, None]).astype(jnp.bfloat16)
    soft_feat = dot1(soft, full_protos).astype(jnp.bfloat16)
    soft_rows = exchange(soft_feat.reshape(n_proto, crops // n_proto, width), PROTO)
    soft_rows = jnp.sum(soft_rows.astype(jnp.float32), axis=0).astype(jnp.bfloat16)
    soft_feat = lax.all_gather(soft_rows, PROTO, axis=0, tiled=True)
    soft_weight = lax.psum_scatter(
        dot0(hidden, soft).astype(jnp.bfloat16), BATCH, scatter_dimension=0, tiled=True
    )
    all_hidden = lax.all_gather(image_hidden, BATCH, axis=0, tiled=True)
    all_hidden = all_hidden.reshape(n_x, 2, images, width).transpose(1, 0, 2, 3)
    all_hidden = all_hidden.reshape(-1, width)

    logits = teacher_scale * products
    weights = jnp.exp(logits - jnp.max(logits, axis=0, keepdims=True))
    for sweep in range(ITERS - 1):
        weights = weights / jnp.sum(weights, axis=0, keepdims=True)
        row_total = total_over_all(jnp.sum(weights, axis=1))
        weights = weights / row_total[:, None]
    weights = weights / jnp.sum(weights, axis=0, keepdims=True)
    row_total = total_over_all(jnp.sum(weights, axis=1))

    cols = weights.shape[1]
    sent = weights.astype(jnp.bfloat16).reshape(2, n_x, images, cols)
    sent = sent.transpose(1, 0, 2, 3).reshape(n_batch, images, cols)
    mine = exchange(sent, BATCH).transpose(1, 0, 2).reshape(images, -1)
    image_feat = dot1(mine, full_protos)
    image_row = jnp.sum(
        exchange(image_feat.reshape(n_proto, images // n_proto, width), PROTO), axis=0
    )
    image_feat = spread(image_row, PROTO).reshape(images, width)
    my_total = lax.dynamic_slice(row_total, (core * half + x_pos * images,), (images,))
    image_feat = student_scale * image_feat / my_total[:, None]
    feat_grad = (
        soft_feat.astype(jnp.float32) - jnp.take(image_feat, assign, axis=0)
    ).astype(jnp.bfloat16)

    targets = (student_scale * (weights / row_total[:, None])).astype(jnp.bfloat16)
    target_weight = dot0(all_hidden, targets).astype(jnp.bfloat16)
    target_weight = exchange(target_weight.reshape(n_batch, -1, cols), BATCH)
    target_weight = target_weight.transpose(1, 0, 2).reshape(-1, n_batch * cols)
    weight_grad = (
        soft_weight.astype(jnp.float32) - target_weight.astype(jnp.float32)
    ).astype(jnp.bfloat16)
    return (feat_grad, weight_grad)


def solution(mesh):
    n_proto, n_batch = mesh.shape["proto"], mesh.shape["batch"]
    side = 1
    while side * side < n_proto:
        side *= 2
    fine = Mesh(
        mesh.devices.reshape(n_proto // side, side, n_batch // 2, 2), ("z", "y", "x", "core")
    )
    return jax.shard_map(
        on_device,
        mesh=fine,
        in_specs=(
            P(BATCH, PROTO),
            P(None, PROTO + BATCH),
            P(BATCH, None),
            P(),
            P(BATCH, PROTO),
            P(BATCH),
            P(BATCH),
        ),
        out_specs=(P(BATCH, None), P(BATCH, PROTO)),
        check_vma=False,
    )
```

```python
import functools

import jax
import jax.numpy as jnp
from jax import lax
from jax.sharding import Mesh, PartitionSpec as P

ITERS = 3

teacher_scale = 3.0
student_scale = 2.0

BATCH = ("x", "core")
PROTO = ("z", "y")


def spread(block, axes):
    count = lax.axis_size(axes)
    return lax.all_to_all(
        jnp.broadcast_to(block[None], (count,) + block.shape),
        axes,
        split_axis=0,
        concat_axis=0,
        tiled=True,
    )


def exchange(parts, axes):
    return lax.all_to_all(parts, axes, split_axis=0, concat_axis=0, tiled=True)


def total_over_all(partial):
    near = jnp.sum(spread(partial, ("z", "core")), axis=0)
    return jnp.sum(spread(near, ("y", "x")), axis=0)


def dot0(left, right):
    return lax.dot_general(
        left, right, (((0,), (0,)), ((), ())), preferred_element_type=jnp.float32
    )


def dot1(left, right):
    return lax.dot_general(
        left, right, (((1,), (1,)), ((), ())), preferred_element_type=jnp.float32
    )


def on_device(
    teacher_feats, teacher_protos, student_feats, crop_table, student_protos, assign, crop_ids
):
    core = lax.axis_index("core")
    n_proto, n_batch = lax.axis_size(PROTO), lax.axis_size(BATCH)
    images, features = teacher_feats.shape
    crops, width = student_feats.shape
    cols = teacher_protos.shape[1]
    swap = [(0, 1), (1, 0)]

    halves = teacher_feats.T.reshape(2, features // 2, images)
    kept = lax.dynamic_index_in_dim(halves, core, keepdims=False)
    given = lax.dynamic_index_in_dim(halves, 1 - core, keepdims=False)
    got = lax.ppermute(given, "core", swap)
    first = core == 0
    rows = jnp.concatenate(
        [jnp.where(first, kept, got), jnp.where(first, got, kept)], axis=1
    )
    rows = spread(rows, PROTO).reshape(-1, 2 * images)
    own_feats = spread(rows, "x")
    other_feats = lax.ppermute(own_feats, "core", swap)
    split = teacher_protos.reshape(n_proto, 2, features // 2, cols)
    own_protos = lax.dynamic_index_in_dim(split, core, axis=1, keepdims=False)
    other_protos = lax.dynamic_index_in_dim(split, 1 - core, axis=1, keepdims=False)
    contract = functools.partial(
        jnp.einsum, "xkr,kn->xrn", preferred_element_type=jnp.float32
    )
    products = contract(own_feats, own_protos.reshape(-1, cols)) + contract(
        other_feats, other_protos.reshape(-1, cols)
    )
    products = products.reshape(-1, cols)

    chosen = (
        crop_ids[:, None] == jnp.arange(crop_table.shape[0], dtype=jnp.int32)[None, :]
    ).astype(jnp.bfloat16)
    table_rows = jnp.dot(chosen, crop_table, preferred_element_type=jnp.float32)
    hidden = (student_feats.astype(jnp.float32) + table_rows).astype(jnp.bfloat16)
    picks = (
        assign[:, None] == jnp.arange(images, dtype=jnp.int32)[None, :]
    ).astype(jnp.bfloat16)
    full_protos = lax.all_gather(student_protos, BATCH, axis=0, tiled=True)
    scores = student_scale * jnp.dot(hidden, full_protos, preferred_element_type=jnp.float32)
    peak = jnp.max(scores, axis=1)
    powers = jnp.exp(scores - peak[:, None])
    power_sum = jnp.sum(powers, axis=1)

    logits = teacher_scale * products
    weights = jnp.exp(logits - jnp.max(logits, axis=0, keepdims=True))
    for sweep in range(ITERS - 1):
        weights = weights / jnp.sum(weights, axis=0, keepdims=True)
        row_total = total_over_all(jnp.sum(weights, axis=1))
        weights = weights / row_total[:, None]
    weights = weights / jnp.sum(weights, axis=0, keepdims=True)

    mine = exchange(weights.reshape(n_batch, images, cols), BATCH)
    partial = jnp.sum(mine, axis=(0, 2))
    seen = spread(jnp.concatenate([partial, peak, power_sum]), PROTO)
    row_total = jnp.sum(seen[:, :images], axis=0)
    peaks, sums = seen[:, images : images + crops], seen[:, images + crops :]
    top = jnp.max(peaks, axis=0)
    denominator = jnp.sum(sums * jnp.exp(peaks - top[None]), axis=0)
    targets = (mine / row_total[None, :, None]).astype(jnp.bfloat16)
    targets = targets.transpose(1, 0, 2).reshape(images, -1)
    crop_targets = jnp.dot(picks, targets, preferred_element_type=jnp.float32)
    probabilities = powers * (jnp.exp(peak - top) / denominator)[:, None]
    logit_grad = (student_scale * (probabilities - crop_targets)).astype(jnp.bfloat16)

    feat_part = dot1(logit_grad, full_protos).astype(jnp.bfloat16)
    feat_rows = exchange(feat_part.reshape(n_proto, crops // n_proto, width), PROTO)
    feat_rows = jnp.sum(feat_rows.astype(jnp.float32), axis=0).astype(jnp.bfloat16)
    feat_grad = spread(feat_rows, PROTO).reshape(crops, width)
    weight_grad = lax.psum_scatter(
        dot0(hidden, logit_grad).astype(jnp.bfloat16), BATCH, scatter_dimension=0, tiled=True
    )
    return (feat_grad, weight_grad)


def solution(mesh):
    n_proto, n_batch = mesh.shape["proto"], mesh.shape["batch"]
    side = 1
    while side * side < n_proto:
        side *= 2
    fine = Mesh(
        mesh.devices.reshape(n_proto // side, side, n_batch // 2, 2), ("z", "y", "x", "core")
    )
    return jax.shard_map(
        on_device,
        mesh=fine,
        in_specs=(
            P(BATCH, PROTO),
            P(None, PROTO + BATCH),
            P(BATCH, None),
            P(),
            P(BATCH, PROTO),
            P(BATCH),
            P(BATCH),
        ),
        out_specs=(P(BATCH, None), P(BATCH, PROTO)),
        check_vma=False,
    )
```

```python
import functools

import jax
import jax.numpy as jnp
from jax import lax
from jax.sharding import Mesh, PartitionSpec as P

ITERS = 3

teacher_scale = 3.0
student_scale = 2.0

BATCH = ("x", "core")
PROTO = ("z", "y")


def spread(block, axes):
    count = lax.axis_size(axes)
    return lax.all_to_all(
        jnp.broadcast_to(block[None], (count,) + block.shape),
        axes,
        split_axis=0,
        concat_axis=0,
        tiled=True,
    )


def exchange(parts, axes):
    return lax.all_to_all(parts, axes, split_axis=0, concat_axis=0, tiled=True)


def dot0(left, right):
    return lax.dot_general(
        left, right, (((0,), (0,)), ((), ())), preferred_element_type=jnp.float32
    )


def dot1(left, right):
    return lax.dot_general(
        left, right, (((1,), (1,)), ((), ())), preferred_element_type=jnp.float32
    )


def on_device(
    teacher_feats, teacher_protos, student_feats, crop_table, student_protos, assign, crop_ids
):
    core = lax.axis_index("core")
    n_proto, n_batch = lax.axis_size(PROTO), lax.axis_size(BATCH)
    images, features = teacher_feats.shape
    crops, width = student_feats.shape
    cols = teacher_protos.shape[1]
    swap = [(0, 1), (1, 0)]

    deep = images // 2
    rows = jnp.concatenate([teacher_feats[:deep], teacher_feats[deep:]], axis=1)
    their_protos = lax.ppermute(teacher_protos, "core", swap)
    rows = spread(rows, PROTO).reshape(n_proto, deep, 2, features)
    rows = rows.transpose(2, 1, 0, 3).reshape(images, -1)
    first = core == 0
    rows, their_protos, first = lax.optimization_barrier((rows, their_protos, first))
    rows = spread(rows, "x")
    rows, student_protos = lax.optimization_barrier((rows, student_protos))
    contract = functools.partial(
        jnp.einsum, "xrk,kn->xrn", preferred_element_type=jnp.float32
    )
    theirs = contract(rows, their_protos)
    own = contract(rows, teacher_protos)
    got = lax.ppermute(theirs, "core", swap)
    products = jnp.stack([jnp.where(first, own, got), jnp.where(first, got, own)], axis=1)
    products = products.reshape(-1, cols)

    picks = (
        assign[:, None] == jnp.arange(images, dtype=jnp.int32)[None, :]
    ).astype(jnp.bfloat16)
    full_protos = lax.all_gather(student_protos, BATCH, axis=0, tiled=True)
    logits = teacher_scale * products
    weights = jnp.exp(logits - jnp.max(logits, axis=0, keepdims=True))
    for sweep in range(ITERS - 1):
        weights = weights / jnp.sum(weights, axis=0, keepdims=True)
        near = jnp.sum(spread(jnp.sum(weights, axis=1), ("z", "core")), axis=0)
        if sweep == ITERS - 2:
            near, full_protos, student_feats, crop_table = lax.optimization_barrier(
                (near, full_protos, student_feats, crop_table)
            )
        row_total = jnp.sum(spread(near, ("y", "x")), axis=0)
        weights = weights / row_total[:, None]
    weights = weights / jnp.sum(weights, axis=0, keepdims=True)

    chosen = (
        crop_ids[:, None] == jnp.arange(crop_table.shape[0], dtype=jnp.int32)[None, :]
    ).astype(jnp.bfloat16)
    table_rows = jnp.dot(chosen, crop_table, preferred_element_type=jnp.float32)
    hidden = (student_feats.astype(jnp.float32) + table_rows).astype(jnp.bfloat16)
    scores = student_scale * jnp.dot(hidden, full_protos, preferred_element_type=jnp.float32)
    peak = jnp.max(scores, axis=1)
    powers = jnp.exp(scores - peak[:, None])
    power_sum = jnp.sum(powers, axis=1)
    soft_feat = dot1(powers.astype(jnp.bfloat16), full_protos)
    weights, powers, soft_feat = lax.optimization_barrier((weights, powers, soft_feat))

    mine = exchange(
        weights.astype(jnp.bfloat16).reshape(n_batch, images, cols), BATCH
    )
    mine = mine.transpose(1, 0, 2).reshape(images, -1)
    partial = jnp.sum(mine.astype(jnp.float32), axis=1)
    image_feat = lax.optimization_barrier(dot1(mine, full_protos))
    seen = spread(jnp.concatenate([partial, peak, power_sum]), PROTO)
    row_total = jnp.sum(seen[:, :images], axis=0)
    peaks, sums = seen[:, images : images + crops], seen[:, images + crops :]
    top = jnp.max(peaks, axis=0)
    denominator = jnp.sum(sums * jnp.exp(peaks - top[None]), axis=0)
    share = jnp.exp(peak - top) / denominator

    image_feat = (image_feat / row_total[:, None]).astype(jnp.bfloat16)
    image_feat = jnp.dot(picks, image_feat, preferred_element_type=jnp.float32)
    feat_part = student_scale * (soft_feat * share[:, None] - image_feat)
    feat_part, share, row_total = lax.optimization_barrier(
        (feat_part.astype(jnp.bfloat16), share, row_total)
    )
    feat_rows = feat_part.reshape(n_proto // 2, -1, 2, width // 2).transpose(0, 2, 1, 3)
    feat_rows = exchange(feat_rows.reshape(n_proto, -1, width // 2), PROTO)
    feat_rows = jnp.sum(feat_rows.astype(jnp.float32), axis=0).astype(jnp.bfloat16)
    feat_grad = spread(feat_rows, PROTO).reshape(n_proto // 2, 2, -1, width // 2)
    feat_grad = feat_grad.transpose(0, 2, 1, 3).reshape(crops, width)

    targets = (mine.astype(jnp.float32) / row_total[:, None]).astype(jnp.bfloat16)
    crop_targets = jnp.dot(picks, targets, preferred_element_type=jnp.float32)
    logit_grad = student_scale * (powers * share[:, None] - crop_targets)
    logit_grad = logit_grad.astype(jnp.bfloat16)
    weight_grad = lax.psum_scatter(
        dot0(hidden, logit_grad).astype(jnp.bfloat16), BATCH, scatter_dimension=0, tiled=True
    )
    return (feat_grad, weight_grad)


def solution(mesh):
    n_proto, n_batch = mesh.shape["proto"], mesh.shape["batch"]
    side = 1
    while side * side < n_proto:
        side *= 2
    fine = Mesh(
        mesh.devices.reshape(n_proto // side, side, n_batch // 2, 2), ("z", "y", "x", "core")
    )
    return jax.shard_map(
        on_device,
        mesh=fine,
        in_specs=(
            P(BATCH, PROTO),
            P(None, PROTO + BATCH),
            P(BATCH, None),
            P(),
            P(BATCH, PROTO),
            P(BATCH),
            P(BATCH),
        ),
        out_specs=(P(BATCH, None), P(BATCH, PROTO)),
        check_vma=False,
    )
```

```python
import jax
import jax.numpy as jnp
from jax import lax
from jax.experimental import pallas as pl
from jax.experimental.pallas import tpu as pltpu
from jax.sharding import Mesh, PartitionSpec as P

ITERS = 3

teacher_scale = 3.0
student_scale = 2.0

BATCH = ("x", "core")
PROTO = ("z", "y")


def spread(block, axes):
    count = lax.axis_size(axes)
    return lax.all_to_all(
        jnp.broadcast_to(block[None], (count,) + block.shape),
        axes,
        split_axis=0,
        concat_axis=0,
        tiled=True,
    )


def exchange(parts, axes):
    return lax.all_to_all(parts, axes, split_axis=0, concat_axis=0, tiled=True)


def dot0(left, right):
    return lax.dot_general(
        left, right, (((0,), (0,)), ((), ())), preferred_element_type=jnp.float32
    )


def dot1(left, right):
    return lax.dot_general(
        left, right, (((1,), (1,)), ((), ())), preferred_element_type=jnp.float32
    )


def unfold_kernel(folded_ref, rows_ref):
    pairs, deep = folded_ref.shape[0] // 2, folded_ref.shape[1]
    lanes = folded_ref.shape[2]
    left = lax.broadcasted_iota(jnp.int32, (deep, lanes), 1) < lanes // 2
    for pair in range(pairs):
        even = folded_ref[2 * pair].astype(jnp.float32)
        odd = folded_ref[2 * pair + 1].astype(jnp.float32)
        upper = jnp.where(left, even, pltpu.roll(odd, lanes // 2, 1))
        lower = jnp.where(left, pltpu.roll(even, lanes // 2, 1), odd)
        columns = pl.ds(pair * lanes, lanes)
        rows_ref[0, 0:deep, columns] = upper.astype(jnp.bfloat16)
        rows_ref[0, deep : 2 * deep, columns] = lower.astype(jnp.bfloat16)


def unfold(folded, copies):
    count, deep, lanes = folded.shape
    width = count * lanes // 2
    return pl.pallas_call(
        unfold_kernel,
        grid=(copies,),
        in_specs=[pl.BlockSpec((count, deep, lanes), lambda i: (0, 0, 0))],
        out_specs=pl.BlockSpec((1, 2 * deep, width), lambda i: (i, 0, 0)),
        out_shape=jax.ShapeDtypeStruct((copies, 2 * deep, width), folded.dtype),
        compiler_params=pltpu.CompilerParams(vmem_limit_bytes=16 * 2**20),
        cost_estimate=pl.CostEstimate(
            flops=0, bytes_accessed=(copies + 1) * folded.size * 2, transcendentals=0
        ),
    )(folded)


def product_kernel(left_ref, right_ref, out_ref):
    part = jnp.dot(left_ref[...], right_ref[...], preferred_element_type=jnp.float32)

    @pl.when(pl.program_id(0) == 0)
    def _():
        out_ref[...] = part

    @pl.when(pl.program_id(0) > 0)
    def _():
        out_ref[...] += part


def product(left, right, steps=4):
    height, depth = left.shape
    width = right.shape[1]
    block = depth // steps
    return pl.pallas_call(
        product_kernel,
        grid=(steps,),
        in_specs=[
            pl.BlockSpec((height, block), lambda k: (0, k)),
            pl.BlockSpec((block, width), lambda k: (k, 0)),
        ],
        out_specs=pl.BlockSpec((height, width), lambda k: (0, 0)),
        out_shape=jax.ShapeDtypeStruct((height, width), jnp.float32),
        compiler_params=pltpu.CompilerParams(vmem_limit_bytes=16 * 2**20),
        cost_estimate=pl.CostEstimate(
            flops=2 * height * width * depth,
            bytes_accessed=2 * (left.size + right.size) + 4 * height * width,
            transcendentals=0,
        ),
    )(left, right)


def on_device(
    teacher_feats, teacher_protos, student_feats, crop_table, student_protos, assign, crop_ids
):
    core = lax.axis_index("core")
    n_proto, n_batch = lax.axis_size(PROTO), lax.axis_size(BATCH)
    images, features = teacher_feats.shape
    crops, width = student_feats.shape
    cols = teacher_protos.shape[1]
    swap = [(0, 1), (1, 0)]

    deep = images // 2
    rows = jnp.concatenate([teacher_feats[:deep], teacher_feats[deep:]], axis=1)
    their_protos = lax.ppermute(teacher_protos, "core", swap)
    rows = exchange(unfold(spread(rows, PROTO), lax.axis_size("x")), "x")

    full_protos = lax.all_gather(student_protos, BATCH, axis=0, tiled=True)
    chosen = (
        crop_ids[:, None] == jnp.arange(crop_table.shape[0], dtype=jnp.int32)[None, :]
    ).astype(jnp.bfloat16)
    table_rows = jnp.dot(chosen, crop_table, preferred_element_type=jnp.float32)
    hidden = (student_feats.astype(jnp.float32) + table_rows).astype(jnp.bfloat16)
    scores = student_scale * jnp.dot(hidden, full_protos, preferred_element_type=jnp.float32)
    peak = jnp.max(scores, axis=1)
    powers = jnp.exp(scores - peak[:, None])
    power_sum = jnp.sum(powers, axis=1)
    soft_feat = dot1(powers.astype(jnp.bfloat16), full_protos)
    rows, powers, peak, power_sum, soft_feat = lax.optimization_barrier(
        (rows, powers, peak, power_sum, soft_feat)
    )

    rows = rows.reshape(-1, rows.shape[2])
    theirs = product(rows, their_protos)
    own = product(rows, teacher_protos)
    got = lax.ppermute(theirs, "core", swap)
    first = core == 0
    own, got = own.reshape(-1, images, cols), got.reshape(-1, images, cols)
    products = jnp.stack([jnp.where(first, own, got), jnp.where(first, got, own)], axis=1)
    products = products.reshape(-1, cols)

    picks = (
        assign[:, None] == jnp.arange(images, dtype=jnp.int32)[None, :]
    ).astype(jnp.bfloat16)
    logits = teacher_scale * products
    weights = jnp.exp(logits - jnp.max(logits, axis=0, keepdims=True))
    for sweep in range(ITERS - 1):
        weights = weights / jnp.sum(weights, axis=0, keepdims=True)
        near = jnp.sum(spread(jnp.sum(weights, axis=1), ("z", "core")), axis=0)
        near, weights = lax.optimization_barrier((near, weights))
        row_total = jnp.sum(spread(near, ("y", "x")), axis=0)
        weights = weights / row_total[:, None]
    weights = weights / jnp.sum(weights, axis=0, keepdims=True)

    mine = exchange(
        weights.astype(jnp.bfloat16).reshape(n_batch, images, cols), BATCH
    )
    mine = mine.transpose(1, 0, 2).reshape(images, -1)
    partial = jnp.sum(mine.astype(jnp.float32), axis=1)
    image_feat = lax.optimization_barrier(dot1(mine, full_protos))
    seen = spread(jnp.concatenate([partial, peak, power_sum]), PROTO)
    row_total = jnp.sum(seen[:, :images], axis=0)
    peaks, sums = seen[:, images : images + crops], seen[:, images + crops :]
    top = jnp.max(peaks, axis=0)
    denominator = jnp.sum(sums * jnp.exp(peaks - top[None]), axis=0)
    share = jnp.exp(peak - top) / denominator

    image_feat = (image_feat / row_total[:, None]).astype(jnp.bfloat16)
    image_feat = jnp.dot(picks, image_feat, preferred_element_type=jnp.float32)
    feat_part = student_scale * (soft_feat * share[:, None] - image_feat)
    feat_part, share, row_total = lax.optimization_barrier(
        (feat_part.astype(jnp.bfloat16), share, row_total)
    )
    feat_rows = feat_part.reshape(n_proto // 2, -1, 2, width // 2).transpose(0, 2, 1, 3)
    feat_rows = exchange(feat_rows.reshape(n_proto, -1, width // 2), PROTO)
    feat_rows = jnp.sum(feat_rows.astype(jnp.float32), axis=0).astype(jnp.bfloat16)
    feat_grad = spread(feat_rows, PROTO).reshape(n_proto // 2, 2, -1, width // 2)
    feat_grad = feat_grad.transpose(0, 2, 1, 3).reshape(crops, width)

    targets = (mine.astype(jnp.float32) / row_total[:, None]).astype(jnp.bfloat16)
    crop_targets = jnp.dot(picks, targets, preferred_element_type=jnp.float32)
    logit_grad = student_scale * (powers * share[:, None] - crop_targets)
    logit_grad = logit_grad.astype(jnp.bfloat16)
    weight_grad = lax.psum_scatter(
        dot0(hidden, logit_grad).astype(jnp.bfloat16), BATCH, scatter_dimension=0, tiled=True
    )
    return (feat_grad, weight_grad)


def solution(mesh):
    n_proto, n_batch = mesh.shape["proto"], mesh.shape["batch"]
    side = 1
    while side * side < n_proto:
        side *= 2
    fine = Mesh(
        mesh.devices.reshape(n_proto // side, side, n_batch // 2, 2), ("z", "y", "x", "core")
    )
    return jax.shard_map(
        on_device,
        mesh=fine,
        in_specs=(
            P(BATCH, PROTO),
            P(None, PROTO + BATCH),
            P(BATCH, None),
            P(),
            P(BATCH, PROTO),
            P(BATCH),
            P(BATCH),
        ),
        out_specs=(P(BATCH, None), P(BATCH, PROTO)),
        check_vma=False,
    )
```

```python
import functools

import jax
import jax.numpy as jnp
from jax import lax
from jax.experimental import pallas as pl
from jax.experimental.pallas import tpu as pltpu
from jax.sharding import Mesh, PartitionSpec as P

ITERS = 3

teacher_scale = 3.0
student_scale = 2.0

BATCH = ("x", "core")
PROTO = ("z", "y")


def spread(block, axes):
    count = lax.axis_size(axes)
    return lax.all_to_all(
        jnp.broadcast_to(block[None], (count,) + block.shape),
        axes,
        split_axis=0,
        concat_axis=0,
        tiled=True,
    )


def exchange(parts, axes):
    return lax.all_to_all(parts, axes, split_axis=0, concat_axis=0, tiled=True)


def dot0(left, right):
    return lax.dot_general(
        left, right, (((0,), (0,)), ((), ())), preferred_element_type=jnp.float32
    )


def dot1(left, right):
    return lax.dot_general(
        left, right, (((1,), (1,)), ((), ())), preferred_element_type=jnp.float32
    )


def unfold_kernel(folded_ref, rows_ref):
    pairs, deep = folded_ref.shape[0] // 2, folded_ref.shape[1]
    lanes = folded_ref.shape[2]
    left = lax.broadcasted_iota(jnp.int32, (deep, lanes), 1) < lanes // 2
    for pair in range(pairs):
        even = folded_ref[2 * pair].astype(jnp.float32)
        odd = folded_ref[2 * pair + 1].astype(jnp.float32)
        upper = jnp.where(left, even, pltpu.roll(odd, lanes // 2, 1))
        lower = jnp.where(left, pltpu.roll(even, lanes // 2, 1), odd)
        columns = pl.ds(pair * lanes, lanes)
        rows_ref[0, 0:deep, columns] = upper.astype(jnp.bfloat16)
        rows_ref[0, deep : 2 * deep, columns] = lower.astype(jnp.bfloat16)


def unfold(folded, copies):
    count, deep, lanes = folded.shape
    width = count * lanes // 2
    return pl.pallas_call(
        unfold_kernel,
        grid=(copies,),
        in_specs=[pl.BlockSpec((count, deep, lanes), lambda i: (0, 0, 0))],
        out_specs=pl.BlockSpec((1, 2 * deep, width), lambda i: (i, 0, 0)),
        out_shape=pltpu.HBM((copies, 2 * deep, width), folded.dtype),
        compiler_params=pltpu.CompilerParams(vmem_limit_bytes=16 * 2**20),
        cost_estimate=pl.CostEstimate(
            flops=0, bytes_accessed=(copies + 1) * folded.size * 2, transcendentals=0
        ),
    )(folded)


def on_device(
    teacher_feats, teacher_protos, student_feats, crop_table, student_protos, assign, crop_ids
):
    core = lax.axis_index("core")
    n_proto, n_batch = lax.axis_size(PROTO), lax.axis_size(BATCH)
    images, features = teacher_feats.shape
    crops, width = student_feats.shape
    cols = teacher_protos.shape[1]
    swap = [(0, 1), (1, 0)]

    deep = images // 2
    rows = jnp.concatenate([teacher_feats[:deep], teacher_feats[deep:]], axis=1)
    their_protos = lax.ppermute(teacher_protos, "core", swap)
    rows, student_protos = lax.optimization_barrier((rows, student_protos))
    rows = exchange(unfold(spread(rows, PROTO), lax.axis_size("x")), "x")

    full_protos = lax.all_gather(student_protos, BATCH, axis=0, tiled=True)
    chosen = (
        crop_ids[:, None] == jnp.arange(crop_table.shape[0], dtype=jnp.int32)[None, :]
    ).astype(jnp.bfloat16)
    table_rows = jnp.dot(chosen, crop_table, preferred_element_type=jnp.float32)
    hidden = (student_feats.astype(jnp.float32) + table_rows).astype(jnp.bfloat16)
    scores = student_scale * jnp.dot(hidden, full_protos, preferred_element_type=jnp.float32)
    peak = jnp.max(scores, axis=1)
    powers = jnp.exp(scores - peak[:, None])
    power_sum = jnp.sum(powers, axis=1)
    soft_feat = dot1(powers.astype(jnp.bfloat16), full_protos)
    rows, powers, peak, power_sum, soft_feat = lax.optimization_barrier(
        (rows, powers, peak, power_sum, soft_feat)
    )

    contract = functools.partial(
        jnp.einsum, "xrk,kn->xrn", preferred_element_type=jnp.float32
    )
    theirs = contract(rows, their_protos)
    own = contract(rows, teacher_protos)
    got = lax.ppermute(theirs, "core", swap)
    first = core == 0
    products = jnp.stack([jnp.where(first, own, got), jnp.where(first, got, own)], axis=1)
    products = products.reshape(-1, cols)

    picks = (
        assign[:, None] == jnp.arange(images, dtype=jnp.int32)[None, :]
    ).astype(jnp.bfloat16)
    logits = teacher_scale * products
    weights = jnp.exp(logits - jnp.max(logits, axis=0, keepdims=True))
    for sweep in range(ITERS - 1):
        weights = weights / jnp.sum(weights, axis=0, keepdims=True)
        near = jnp.sum(spread(jnp.sum(weights, axis=1), ("z", "core")), axis=0)
        if sweep == ITERS - 2:
            near, weights = lax.optimization_barrier((near, weights))
        row_total = jnp.sum(spread(near, ("y", "x")), axis=0)
        weights = weights / row_total[:, None]
    weights = weights / jnp.sum(weights, axis=0, keepdims=True)

    mine = exchange(
        weights.astype(jnp.bfloat16).reshape(n_batch, images, cols), BATCH
    )
    mine = mine.transpose(1, 0, 2).reshape(images, -1)
    partial = jnp.sum(mine.astype(jnp.float32), axis=1)
    image_feat = lax.optimization_barrier(dot1(mine, full_protos))
    seen = spread(jnp.concatenate([partial, peak, power_sum]), PROTO)
    row_total = jnp.sum(seen[:, :images], axis=0)
    peaks, sums = seen[:, images : images + crops], seen[:, images + crops :]
    top = jnp.max(peaks, axis=0)
    denominator = jnp.sum(sums * jnp.exp(peaks - top[None]), axis=0)
    share = jnp.exp(peak - top) / denominator

    image_feat = (image_feat / row_total[:, None]).astype(jnp.bfloat16)
    image_feat = jnp.dot(picks, image_feat, preferred_element_type=jnp.float32)
    feat_part = student_scale * (soft_feat * share[:, None] - image_feat)
    feat_part, share, row_total = lax.optimization_barrier(
        (feat_part.astype(jnp.bfloat16), share, row_total)
    )
    feat_rows = feat_part.reshape(n_proto // 2, -1, 2, width // 2).transpose(0, 2, 1, 3)
    feat_rows = exchange(feat_rows.reshape(n_proto, -1, width // 2), PROTO)
    feat_rows = jnp.sum(feat_rows.astype(jnp.float32), axis=0).astype(jnp.bfloat16)
    feat_grad = spread(feat_rows, PROTO).reshape(n_proto // 2, 2, -1, width // 2)
    feat_grad = feat_grad.transpose(0, 2, 1, 3).reshape(crops, width)

    targets = (mine.astype(jnp.float32) / row_total[:, None]).astype(jnp.bfloat16)
    crop_targets = jnp.dot(picks, targets, preferred_element_type=jnp.float32)
    logit_grad = student_scale * (powers * share[:, None] - crop_targets)
    logit_grad = logit_grad.astype(jnp.bfloat16)
    weight_grad = lax.psum_scatter(
        dot0(hidden, logit_grad).astype(jnp.bfloat16), BATCH, scatter_dimension=0, tiled=True
    )
    return (feat_grad, weight_grad)


def solution(mesh):
    n_proto, n_batch = mesh.shape["proto"], mesh.shape["batch"]
    side = 1
    while side * side < n_proto:
        side *= 2
    fine = Mesh(
        mesh.devices.reshape(n_proto // side, side, n_batch // 2, 2), ("z", "y", "x", "core")
    )
    return jax.shard_map(
        on_device,
        mesh=fine,
        in_specs=(
            P(BATCH, PROTO),
            P(None, PROTO + BATCH),
            P(BATCH, None),
            P(),
            P(BATCH, PROTO),
            P(BATCH),
            P(BATCH),
        ),
        out_specs=(P(BATCH, None), P(BATCH, PROTO)),
        check_vma=False,
    )
```

```python
import functools

import jax
import jax.numpy as jnp
from jax import lax
from jax.experimental import pallas as pl
from jax.experimental.pallas import tpu as pltpu
from jax.sharding import Mesh, PartitionSpec as P

ITERS = 3

teacher_scale = 3.0
student_scale = 2.0

BATCH = ("x", "core")
PROTO = ("z", "y")


def spread(block, axes):
    count = lax.axis_size(axes)
    return lax.all_to_all(
        jnp.broadcast_to(block[None], (count,) + block.shape),
        axes,
        split_axis=0,
        concat_axis=0,
        tiled=True,
    )


def exchange(parts, axes):
    return lax.all_to_all(parts, axes, split_axis=0, concat_axis=0, tiled=True)


def dot0(left, right):
    return lax.dot_general(
        left, right, (((0,), (0,)), ((), ())), preferred_element_type=jnp.float32
    )


def dot1(left, right):
    return lax.dot_general(
        left, right, (((1,), (1,)), ((), ())), preferred_element_type=jnp.float32
    )


def unfold_kernel(folded_ref, rows_ref):
    pairs, deep = folded_ref.shape[0] // 2, folded_ref.shape[1]
    lanes = folded_ref.shape[2]
    left = lax.broadcasted_iota(jnp.int32, (deep, lanes), 1) < lanes // 2
    for pair in range(pairs):
        even = folded_ref[2 * pair].astype(jnp.float32)
        odd = folded_ref[2 * pair + 1].astype(jnp.float32)
        upper = jnp.where(left, even, pltpu.roll(odd, lanes // 2, 1))
        lower = jnp.where(left, pltpu.roll(even, lanes // 2, 1), odd)
        columns = pl.ds(pair * lanes, lanes)
        rows_ref[0, 0:deep, columns] = upper.astype(jnp.bfloat16)
        rows_ref[0, deep : 2 * deep, columns] = lower.astype(jnp.bfloat16)


def unfold(folded, copies):
    count, deep, lanes = folded.shape
    width = count * lanes // 2
    return pl.pallas_call(
        unfold_kernel,
        grid=(copies,),
        in_specs=[pl.BlockSpec((count, deep, lanes), lambda i: (0, 0, 0))],
        out_specs=pl.BlockSpec((1, 2 * deep, width), lambda i: (i, 0, 0)),
        out_shape=pltpu.HBM((copies, 2 * deep, width), folded.dtype),
        compiler_params=pltpu.CompilerParams(vmem_limit_bytes=16 * 2**20),
        cost_estimate=pl.CostEstimate(
            flops=0, bytes_accessed=(copies + 1) * folded.size * 2, transcendentals=0
        ),
    )(folded)


def on_device(
    teacher_feats, teacher_protos, student_feats, crop_table, student_protos, assign, crop_ids
):
    core = lax.axis_index("core")
    n_proto, n_batch = lax.axis_size(PROTO), lax.axis_size(BATCH)
    images, features = teacher_feats.shape
    crops, width = student_feats.shape
    cols = teacher_protos.shape[1]
    swap = [(0, 1), (1, 0)]

    deep = images // 2
    rows = jnp.concatenate([teacher_feats[:deep], teacher_feats[deep:]], axis=1)
    their_protos = lax.ppermute(teacher_protos, "core", swap)
    rows, student_protos = lax.optimization_barrier((rows, student_protos))
    rows = exchange(unfold(spread(rows, PROTO), lax.axis_size("x")), "x")

    full_protos = lax.all_gather(student_protos, BATCH, axis=0, tiled=True)
    chosen = (
        crop_ids[:, None] == jnp.arange(crop_table.shape[0], dtype=jnp.int32)[None, :]
    ).astype(jnp.bfloat16)
    table_rows = jnp.dot(chosen, crop_table, preferred_element_type=jnp.float32)
    hidden = (student_feats.astype(jnp.float32) + table_rows).astype(jnp.bfloat16)
    scores = student_scale * jnp.dot(hidden, full_protos, preferred_element_type=jnp.float32)
    peak = jnp.max(scores, axis=1)
    powers = jnp.exp(scores - peak[:, None])
    power_sum = jnp.sum(powers, axis=1)
    rows, powers, peak, power_sum = lax.optimization_barrier(
        (rows, powers, peak, power_sum)
    )

    contract = functools.partial(
        jnp.einsum, "xrk,kn->xrn", preferred_element_type=jnp.float32
    )
    theirs = contract(rows, their_protos)
    own = contract(rows, teacher_protos)
    got = lax.ppermute(theirs, "core", swap)
    first = core == 0
    products = jnp.stack([jnp.where(first, own, got), jnp.where(first, got, own)], axis=1)
    products = products.reshape(-1, cols)

    picks = (
        assign[:, None] == jnp.arange(images, dtype=jnp.int32)[None, :]
    ).astype(jnp.bfloat16)
    logits = teacher_scale * products
    weights = jnp.exp(logits - jnp.max(logits, axis=0, keepdims=True))
    for sweep in range(ITERS - 1):
        weights = lax.optimization_barrier(
            weights / jnp.sum(weights, axis=0, keepdims=True)
        )
        near = jnp.sum(spread(jnp.sum(weights, axis=1), ("z", "core")), axis=0)
        row_total = jnp.sum(spread(near, ("y", "x")), axis=0)
        weights = weights / row_total[:, None]
    weights = weights / jnp.sum(weights, axis=0, keepdims=True)

    mine = exchange(
        weights.astype(jnp.bfloat16).reshape(n_batch, images, cols), BATCH
    )
    mine = mine.transpose(1, 0, 2).reshape(images, -1)
    partial = jnp.sum(mine.astype(jnp.float32), axis=1)
    seen = spread(jnp.concatenate([partial, peak, power_sum]), PROTO)
    row_total = jnp.sum(seen[:, :images], axis=0)
    peaks, sums = seen[:, images : images + crops], seen[:, images + crops :]
    top = jnp.max(peaks, axis=0)
    denominator = jnp.sum(sums * jnp.exp(peaks - top[None]), axis=0)
    share = jnp.exp(peak - top) / denominator

    targets = (mine.astype(jnp.float32) / row_total[:, None]).astype(jnp.bfloat16)
    crop_targets = jnp.dot(picks, targets, preferred_element_type=jnp.float32)
    logit_grad = student_scale * (powers * share[:, None] - crop_targets)
    logit_grad = lax.optimization_barrier(logit_grad.astype(jnp.bfloat16))

    feat_part = dot1(logit_grad, full_protos).astype(jnp.bfloat16)
    feat_rows = feat_part.reshape(n_proto // 2, -1, 2, width // 2).transpose(0, 2, 1, 3)
    feat_rows = exchange(feat_rows.reshape(n_proto, -1, width // 2), PROTO)
    feat_rows = jnp.sum(feat_rows.astype(jnp.float32), axis=0).astype(jnp.bfloat16)
    feat_grad = spread(feat_rows, PROTO).reshape(n_proto // 2, 2, -1, width // 2)
    feat_grad = feat_grad.transpose(0, 2, 1, 3).reshape(crops, width)

    weight_grad = lax.psum_scatter(
        dot0(hidden, logit_grad).astype(jnp.bfloat16), BATCH, scatter_dimension=0, tiled=True
    )
    return (feat_grad, weight_grad)


def solution(mesh):
    n_proto, n_batch = mesh.shape["proto"], mesh.shape["batch"]
    side = 1
    while side * side < n_proto:
        side *= 2
    fine = Mesh(
        mesh.devices.reshape(n_proto // side, side, n_batch // 2, 2), ("z", "y", "x", "core")
    )
    return jax.shard_map(
        on_device,
        mesh=fine,
        in_specs=(
            P(BATCH, PROTO),
            P(None, PROTO + BATCH),
            P(BATCH, None),
            P(),
            P(BATCH, PROTO),
            P(BATCH),
            P(BATCH),
        ),
        out_specs=(P(BATCH, None), P(BATCH, PROTO)),
        check_vma=False,
    )
```

```python
import functools

import jax
import jax.numpy as jnp
from jax import lax
from jax.experimental import pallas as pl
from jax.experimental.pallas import tpu as pltpu
from jax.sharding import Mesh, PartitionSpec as P

ITERS = 3

teacher_scale = 3.0
student_scale = 2.0

BATCH = ("x", "core")
PROTO = ("z", "y")


def spread(block, axes):
    count = lax.axis_size(axes)
    return lax.all_to_all(
        jnp.broadcast_to(block[None], (count,) + block.shape),
        axes,
        split_axis=0,
        concat_axis=0,
        tiled=True,
    )


def exchange(parts, axes):
    return lax.all_to_all(parts, axes, split_axis=0, concat_axis=0, tiled=True)


def dot0(left, right):
    return lax.dot_general(
        left, right, (((0,), (0,)), ((), ())), preferred_element_type=jnp.float32
    )


def dot1(left, right):
    return lax.dot_general(
        left, right, (((1,), (1,)), ((), ())), preferred_element_type=jnp.float32
    )


def unfold_kernel(folded_ref, rows_ref):
    pairs, deep = folded_ref.shape[0] // 2, folded_ref.shape[1]
    lanes = folded_ref.shape[2]
    left = lax.broadcasted_iota(jnp.int32, (deep, lanes), 1) < lanes // 2
    for pair in range(pairs):
        even = folded_ref[2 * pair].astype(jnp.float32)
        odd = folded_ref[2 * pair + 1].astype(jnp.float32)
        upper = jnp.where(left, even, pltpu.roll(odd, lanes // 2, 1))
        lower = jnp.where(left, pltpu.roll(even, lanes // 2, 1), odd)
        columns = pl.ds(pair * lanes, lanes)
        rows_ref[0, 0:deep, columns] = upper.astype(jnp.bfloat16)
        rows_ref[0, deep : 2 * deep, columns] = lower.astype(jnp.bfloat16)


def unfold(folded, copies):
    count, deep, lanes = folded.shape
    width = count * lanes // 2
    return pl.pallas_call(
        unfold_kernel,
        grid=(copies,),
        in_specs=[pl.BlockSpec((count, deep, lanes), lambda i: (0, 0, 0))],
        out_specs=pl.BlockSpec((1, 2 * deep, width), lambda i: (i, 0, 0)),
        out_shape=pltpu.HBM((copies, 2 * deep, width), folded.dtype),
        compiler_params=pltpu.CompilerParams(vmem_limit_bytes=16 * 2**20),
        cost_estimate=pl.CostEstimate(
            flops=0, bytes_accessed=(copies + 1) * folded.size * 2, transcendentals=0
        ),
    )(folded)


def on_device(
    teacher_feats, teacher_protos, student_feats, crop_table, student_protos, assign, crop_ids
):
    core = lax.axis_index("core")
    n_proto, n_batch = lax.axis_size(PROTO), lax.axis_size(BATCH)
    images, features = teacher_feats.shape
    crops, width = student_feats.shape
    cols = teacher_protos.shape[1]
    swap = [(0, 1), (1, 0)]

    deep = images // 2
    rows = jnp.concatenate([teacher_feats[:deep], teacher_feats[deep:]], axis=1)
    their_protos = lax.ppermute(teacher_protos, "core", swap)
    rows = exchange(unfold(spread(rows, PROTO), lax.axis_size("x")), "x")
    rows, student_protos = lax.optimization_barrier((rows, student_protos))
    full_protos = lax.all_gather(student_protos, BATCH, axis=0, tiled=True)

    contract = functools.partial(
        jnp.einsum, "xrk,kn->xrn", preferred_element_type=jnp.float32
    )
    theirs = contract(rows, their_protos)
    own = contract(rows, teacher_protos)
    got = lax.ppermute(theirs, "core", swap)
    first = core == 0
    products = jnp.stack([jnp.where(first, own, got), jnp.where(first, got, own)], axis=1)
    products = products.reshape(-1, cols)

    picks = (
        assign[:, None] == jnp.arange(images, dtype=jnp.int32)[None, :]
    ).astype(jnp.bfloat16)
    logits = teacher_scale * products
    weights = jnp.exp(logits - jnp.max(logits, axis=0, keepdims=True))
    for sweep in range(ITERS - 1):
        weights = lax.optimization_barrier(
            weights / jnp.sum(weights, axis=0, keepdims=True)
        )
        near = jnp.sum(spread(jnp.sum(weights, axis=1), ("z", "core")), axis=0)
        row_total = jnp.sum(spread(near, ("y", "x")), axis=0)
        if sweep == ITERS - 2:
            row_total, full_protos, student_feats, crop_table = lax.optimization_barrier(
                (row_total, full_protos, student_feats, crop_table)
            )
        weights = weights / row_total[:, None]
    weights = weights / jnp.sum(weights, axis=0, keepdims=True)

    chosen = (
        crop_ids[:, None] == jnp.arange(crop_table.shape[0], dtype=jnp.int32)[None, :]
    ).astype(jnp.bfloat16)
    table_rows = jnp.dot(chosen, crop_table, preferred_element_type=jnp.float32)
    hidden = (student_feats.astype(jnp.float32) + table_rows).astype(jnp.bfloat16)
    scores = student_scale * jnp.dot(hidden, full_protos, preferred_element_type=jnp.float32)
    peak = jnp.max(scores, axis=1)
    powers = jnp.exp(scores - peak[:, None])
    power_sum = jnp.sum(powers, axis=1)

    mine = exchange(
        weights.astype(jnp.bfloat16).reshape(n_batch, images, cols), BATCH
    )
    mine = mine.transpose(1, 0, 2).reshape(images, -1)
    partial = jnp.sum(mine.astype(jnp.float32), axis=1)
    seen = spread(jnp.concatenate([partial, peak, power_sum]), PROTO)
    row_total = jnp.sum(seen[:, :images], axis=0)
    peaks, sums = seen[:, images : images + crops], seen[:, images + crops :]
    top = jnp.max(peaks, axis=0)
    denominator = jnp.sum(sums * jnp.exp(peaks - top[None]), axis=0)
    share = jnp.exp(peak - top) / denominator

    targets = (mine.astype(jnp.float32) / row_total[:, None]).astype(jnp.bfloat16)
    crop_targets = jnp.dot(picks, targets, preferred_element_type=jnp.float32)
    logit_grad = student_scale * (powers * share[:, None] - crop_targets)
    logit_grad = logit_grad.astype(jnp.bfloat16)

    feat_part = dot1(logit_grad, full_protos).astype(jnp.bfloat16)
    feat_rows = feat_part.reshape(n_proto // 2, -1, 2, width // 2).transpose(0, 2, 1, 3)
    feat_rows = exchange(feat_rows.reshape(n_proto, -1, width // 2), PROTO)
    feat_rows = jnp.sum(feat_rows.astype(jnp.float32), axis=0).astype(jnp.bfloat16)
    feat_grad = spread(feat_rows, PROTO).reshape(n_proto // 2, 2, -1, width // 2)
    feat_grad = feat_grad.transpose(0, 2, 1, 3).reshape(crops, width)

    weight_grad = lax.psum_scatter(
        dot0(hidden, logit_grad).astype(jnp.bfloat16), BATCH, scatter_dimension=0, tiled=True
    )
    return (feat_grad, weight_grad)


def solution(mesh):
    n_proto, n_batch = mesh.shape["proto"], mesh.shape["batch"]
    side = 1
    while side * side < n_proto:
        side *= 2
    fine = Mesh(
        mesh.devices.reshape(n_proto // side, side, n_batch // 2, 2), ("z", "y", "x", "core")
    )
    return jax.shard_map(
        on_device,
        mesh=fine,
        in_specs=(
            P(BATCH, PROTO),
            P(None, PROTO + BATCH),
            P(BATCH, None),
            P(),
            P(BATCH, PROTO),
            P(BATCH),
            P(BATCH),
        ),
        out_specs=(P(BATCH, None), P(BATCH, PROTO)),
        check_vma=False,
    )
```

```python
import functools

import jax
import jax.numpy as jnp
from jax import lax
from jax.experimental import pallas as pl
from jax.experimental.pallas import tpu as pltpu
from jax.sharding import Mesh, PartitionSpec as P

ITERS = 3

teacher_scale = 3.0
student_scale = 2.0

BATCH = ("x", "core")
PROTO = ("z", "y")


def spread(block, axes):
    count = lax.axis_size(axes)
    return lax.all_to_all(
        jnp.broadcast_to(block[None], (count,) + block.shape),
        axes,
        split_axis=0,
        concat_axis=0,
        tiled=True,
    )


def exchange(parts, axes):
    return lax.all_to_all(parts, axes, split_axis=0, concat_axis=0, tiled=True)


def dot0(left, right):
    return lax.dot_general(
        left, right, (((0,), (0,)), ((), ())), preferred_element_type=jnp.float32
    )


def dot1(left, right):
    return lax.dot_general(
        left, right, (((1,), (1,)), ((), ())), preferred_element_type=jnp.float32
    )


def unfold_kernel(folded_ref, rows_ref):
    pairs, deep = folded_ref.shape[0] // 2, folded_ref.shape[1]
    lanes = folded_ref.shape[2]
    left = lax.broadcasted_iota(jnp.int32, (deep, lanes), 1) < lanes // 2
    for pair in range(pairs):
        even = folded_ref[2 * pair].astype(jnp.float32)
        odd = folded_ref[2 * pair + 1].astype(jnp.float32)
        upper = jnp.where(left, even, pltpu.roll(odd, lanes // 2, 1))
        lower = jnp.where(left, pltpu.roll(even, lanes // 2, 1), odd)
        columns = pl.ds(pair * lanes, lanes)
        rows_ref[0, 0:deep, columns] = upper.astype(jnp.bfloat16)
        rows_ref[0, deep : 2 * deep, columns] = lower.astype(jnp.bfloat16)


def unfold(folded, copies):
    count, deep, lanes = folded.shape
    width = count * lanes // 2
    return pl.pallas_call(
        unfold_kernel,
        grid=(copies,),
        in_specs=[pl.BlockSpec((count, deep, lanes), lambda i: (0, 0, 0))],
        out_specs=pl.BlockSpec((1, 2 * deep, width), lambda i: (i, 0, 0)),
        out_shape=pltpu.HBM((copies, 2 * deep, width), folded.dtype),
        compiler_params=pltpu.CompilerParams(vmem_limit_bytes=16 * 2**20),
        cost_estimate=pl.CostEstimate(
            flops=0, bytes_accessed=(copies + 1) * folded.size * 2, transcendentals=0
        ),
    )(folded)


def on_device(
    teacher_feats, teacher_protos, student_feats, crop_table, student_protos, assign, crop_ids
):
    core = lax.axis_index("core")
    n_proto, n_batch = lax.axis_size(PROTO), lax.axis_size(BATCH)
    images, features = teacher_feats.shape
    crops, width = student_feats.shape
    cols = teacher_protos.shape[1]
    swap = [(0, 1), (1, 0)]

    deep = images // 2
    rows = jnp.concatenate([teacher_feats[:deep], teacher_feats[deep:]], axis=1)
    their_protos = lax.ppermute(teacher_protos, "core", swap)
    rows = spread(rows, PROTO)
    rows, their_protos = lax.optimization_barrier((rows, their_protos))
    rows = exchange(unfold(rows, lax.axis_size("x")), "x")
    rows, student_protos = lax.optimization_barrier((rows, student_protos))
    full_protos = lax.all_gather(student_protos, BATCH, axis=0, tiled=True)

    contract = functools.partial(
        jnp.einsum, "xrk,kn->xrn", preferred_element_type=jnp.float32
    )
    theirs = contract(rows, their_protos)
    own = contract(rows, teacher_protos)
    got = lax.ppermute(theirs, "core", swap)
    first = core == 0
    products = jnp.stack([jnp.where(first, own, got), jnp.where(first, got, own)], axis=1)
    products = products.reshape(-1, cols)

    picks = (
        assign[:, None] == jnp.arange(images, dtype=jnp.int32)[None, :]
    ).astype(jnp.bfloat16)
    logits = teacher_scale * products
    weights = jnp.exp(logits - jnp.max(logits, axis=0, keepdims=True))
    for sweep in range(ITERS - 1):
        weights = lax.optimization_barrier(
            weights / jnp.sum(weights, axis=0, keepdims=True)
        )
        near = jnp.sum(spread(jnp.sum(weights, axis=1), ("z", "core")), axis=0)
        row_total = jnp.sum(spread(near, ("y", "x")), axis=0)
        if sweep == ITERS - 2:
            row_total, full_protos, student_feats, crop_table = lax.optimization_barrier(
                (row_total, full_protos, student_feats, crop_table)
            )
        weights = weights / row_total[:, None]
    weights = weights / jnp.sum(weights, axis=0, keepdims=True)

    chosen = (
        crop_ids[:, None] == jnp.arange(crop_table.shape[0], dtype=jnp.int32)[None, :]
    ).astype(jnp.bfloat16)
    table_rows = jnp.dot(chosen, crop_table, preferred_element_type=jnp.float32)
    hidden = (student_feats.astype(jnp.float32) + table_rows).astype(jnp.bfloat16)
    scores = student_scale * jnp.dot(hidden, full_protos, preferred_element_type=jnp.float32)
    peak = jnp.max(scores, axis=1)
    powers = jnp.exp(scores - peak[:, None])
    power_sum = jnp.sum(powers, axis=1)

    mine = exchange(
        weights.astype(jnp.bfloat16).reshape(n_batch, images, cols), BATCH
    )
    mine = mine.transpose(1, 0, 2).reshape(images, -1)
    partial = jnp.sum(mine.astype(jnp.float32), axis=1)
    seen = spread(jnp.concatenate([partial, peak, power_sum]), PROTO)
    row_total = jnp.sum(seen[:, :images], axis=0)
    peaks, sums = seen[:, images : images + crops], seen[:, images + crops :]
    top = jnp.max(peaks, axis=0)
    denominator = jnp.sum(sums * jnp.exp(peaks - top[None]), axis=0)
    share = jnp.exp(peak - top) / denominator

    targets = (mine.astype(jnp.float32) / row_total[:, None]).astype(jnp.bfloat16)
    crop_targets = jnp.dot(picks, targets, preferred_element_type=jnp.float32)
    logit_grad = student_scale * (powers * share[:, None] - crop_targets)
    logit_grad = logit_grad.astype(jnp.bfloat16)

    feat_part = dot1(logit_grad, full_protos).astype(jnp.bfloat16)
    feat_part, logit_grad = lax.optimization_barrier((feat_part, logit_grad))
    feat_rows = feat_part.reshape(n_proto // 2, -1, 2, width // 2).transpose(0, 2, 1, 3)
    feat_rows = exchange(feat_rows.reshape(n_proto, -1, width // 2), PROTO)
    feat_rows = jnp.sum(feat_rows.astype(jnp.float32), axis=0).astype(jnp.bfloat16)
    feat_grad = spread(feat_rows, PROTO).reshape(n_proto // 2, 2, -1, width // 2)
    feat_grad = feat_grad.transpose(0, 2, 1, 3).reshape(crops, width)

    weight_grad = lax.psum_scatter(
        dot0(hidden, logit_grad).astype(jnp.bfloat16), BATCH, scatter_dimension=0, tiled=True
    )
    return (feat_grad, weight_grad)


def solution(mesh):
    n_proto, n_batch = mesh.shape["proto"], mesh.shape["batch"]
    side = 1
    while side * side < n_proto:
        side *= 2
    fine = Mesh(
        mesh.devices.reshape(n_proto // side, side, n_batch // 2, 2), ("z", "y", "x", "core")
    )
    return jax.shard_map(
        on_device,
        mesh=fine,
        in_specs=(
            P(BATCH, PROTO),
            P(None, PROTO + BATCH),
            P(BATCH, None),
            P(),
            P(BATCH, PROTO),
            P(BATCH),
            P(BATCH),
        ),
        out_specs=(P(BATCH, None), P(BATCH, PROTO)),
        check_vma=False,
    )
```

```python
import functools

import jax
import jax.numpy as jnp
from jax import lax
from jax.experimental import pallas as pl
from jax.experimental.pallas import tpu as pltpu
from jax.sharding import Mesh, PartitionSpec as P

ITERS = 3

teacher_scale = 3.0
student_scale = 2.0

BATCH = ("x", "core")
PROTO = ("z", "y")


def spread(block, axes):
    count = lax.axis_size(axes)
    return lax.all_to_all(
        jnp.broadcast_to(block[None], (count,) + block.shape),
        axes,
        split_axis=0,
        concat_axis=0,
        tiled=True,
    )


def exchange(parts, axes):
    return lax.all_to_all(parts, axes, split_axis=0, concat_axis=0, tiled=True)


def dot0(left, right):
    return lax.dot_general(
        left, right, (((0,), (0,)), ((), ())), preferred_element_type=jnp.float32
    )


def dot1(left, right):
    return lax.dot_general(
        left, right, (((1,), (1,)), ((), ())), preferred_element_type=jnp.float32
    )


def unfold_kernel(folded_ref, rows_ref):
    pairs, deep = folded_ref.shape[0] // 2, folded_ref.shape[1]
    lanes = folded_ref.shape[2]
    left = lax.broadcasted_iota(jnp.int32, (deep, lanes), 1) < lanes // 2
    for pair in range(pairs):
        even = folded_ref[2 * pair].astype(jnp.float32)
        odd = folded_ref[2 * pair + 1].astype(jnp.float32)
        upper = jnp.where(left, even, pltpu.roll(odd, lanes // 2, 1))
        lower = jnp.where(left, pltpu.roll(even, lanes // 2, 1), odd)
        columns = pl.ds(pair * lanes, lanes)
        rows_ref[0, 0:deep, columns] = upper.astype(jnp.bfloat16)
        rows_ref[0, deep : 2 * deep, columns] = lower.astype(jnp.bfloat16)


def unfold(folded, copies):
    count, deep, lanes = folded.shape
    width = count * lanes // 2
    return pl.pallas_call(
        unfold_kernel,
        grid=(copies,),
        in_specs=[pl.BlockSpec((count, deep, lanes), lambda i: (0, 0, 0))],
        out_specs=pl.BlockSpec((1, 2 * deep, width), lambda i: (i, 0, 0)),
        out_shape=jax.ShapeDtypeStruct((copies, 2 * deep, width), folded.dtype),
        compiler_params=pltpu.CompilerParams(vmem_limit_bytes=16 * 2**20),
        cost_estimate=pl.CostEstimate(
            flops=0, bytes_accessed=(copies + 1) * folded.size * 2, transcendentals=0
        ),
    )(folded)


def on_device(
    teacher_feats, teacher_protos, student_feats, crop_table, student_protos, assign, crop_ids
):
    core = lax.axis_index("core")
    n_proto, n_batch = lax.axis_size(PROTO), lax.axis_size(BATCH)
    images, features = teacher_feats.shape
    crops, width = student_feats.shape
    cols = teacher_protos.shape[1]
    swap = [(0, 1), (1, 0)]

    deep = images // 2
    rows = jnp.concatenate([teacher_feats[:deep], teacher_feats[deep:]], axis=1)
    their_protos = lax.ppermute(teacher_protos, "core", swap)
    rows = spread(rows, PROTO)
    rows, their_protos = lax.optimization_barrier((rows, their_protos))
    rows = exchange(unfold(rows, lax.axis_size("x")), "x")
    rows, student_protos = lax.optimization_barrier((rows, student_protos))
    full_protos = lax.all_gather(student_protos, BATCH, axis=0, tiled=True)

    contract = functools.partial(
        jnp.einsum, "xrk,kn->xrn", preferred_element_type=jnp.float32
    )
    theirs = contract(rows, their_protos)
    own = contract(rows, teacher_protos)
    got = lax.ppermute(theirs, "core", swap)
    first = core == 0
    products = jnp.stack([jnp.where(first, own, got), jnp.where(first, got, own)], axis=1)
    products = products.reshape(-1, cols)

    picks = (
        assign[:, None] == jnp.arange(images, dtype=jnp.int32)[None, :]
    ).astype(jnp.bfloat16)
    logits = teacher_scale * products
    weights = jnp.exp(logits - jnp.max(logits, axis=0, keepdims=True))
    for sweep in range(ITERS - 1):
        weights = lax.optimization_barrier(
            weights / jnp.sum(weights, axis=0, keepdims=True)
        )
        near = jnp.sum(spread(jnp.sum(weights, axis=1), ("z", "core")), axis=0)
        row_total = jnp.sum(spread(near, ("y", "x")), axis=0)
        if sweep == ITERS - 2:
            row_total, full_protos, student_feats, crop_table = lax.optimization_barrier(
                (row_total, full_protos, student_feats, crop_table)
            )
        weights = weights / row_total[:, None]
    weights = weights / jnp.sum(weights, axis=0, keepdims=True)

    chosen = (
        crop_ids[:, None] == jnp.arange(crop_table.shape[0], dtype=jnp.int32)[None, :]
    ).astype(jnp.bfloat16)
    table_rows = jnp.dot(chosen, crop_table, preferred_element_type=jnp.float32)
    hidden = (student_feats.astype(jnp.float32) + table_rows).astype(jnp.bfloat16)
    scores = student_scale * jnp.dot(hidden, full_protos, preferred_element_type=jnp.float32)
    peak = jnp.max(scores, axis=1)
    powers = jnp.exp(scores - peak[:, None])
    power_sum = jnp.sum(powers, axis=1)

    mine = exchange(
        weights.astype(jnp.bfloat16).reshape(n_batch, images, cols), BATCH
    )
    mine = mine.transpose(1, 0, 2).reshape(images, -1)
    partial = jnp.sum(mine.astype(jnp.float32), axis=1)
    seen = spread(jnp.concatenate([partial, peak, power_sum]), PROTO)
    row_total = jnp.sum(seen[:, :images], axis=0)
    peaks, sums = seen[:, images : images + crops], seen[:, images + crops :]
    top = jnp.max(peaks, axis=0)
    denominator = jnp.sum(sums * jnp.exp(peaks - top[None]), axis=0)
    share = jnp.exp(peak - top) / denominator

    targets = (mine.astype(jnp.float32) / row_total[:, None]).astype(jnp.bfloat16)
    crop_targets = jnp.dot(picks, targets, preferred_element_type=jnp.float32)
    logit_grad = student_scale * (powers * share[:, None] - crop_targets)
    logit_grad = logit_grad.astype(jnp.bfloat16)

    feat_part = dot1(logit_grad, full_protos).astype(jnp.bfloat16)
    feat_part, logit_grad = lax.optimization_barrier((feat_part, logit_grad))
    feat_rows = feat_part.reshape(n_proto // 2, -1, 2, width // 2).transpose(0, 2, 1, 3)
    feat_rows = exchange(feat_rows.reshape(n_proto, -1, width // 2), PROTO)
    feat_rows = jnp.sum(feat_rows.astype(jnp.float32), axis=0).astype(jnp.bfloat16)
    feat_grad = spread(feat_rows, PROTO).reshape(n_proto // 2, 2, -1, width // 2)
    feat_grad = feat_grad.transpose(0, 2, 1, 3).reshape(crops, width)

    weight_grad = lax.psum_scatter(
        dot0(hidden, logit_grad).astype(jnp.bfloat16), BATCH, scatter_dimension=0, tiled=True
    )
    return (feat_grad, weight_grad)


def solution(mesh):
    n_proto, n_batch = mesh.shape["proto"], mesh.shape["batch"]
    side = 1
    while side * side < n_proto:
        side *= 2
    fine = Mesh(
        mesh.devices.reshape(n_proto // side, side, n_batch // 2, 2), ("z", "y", "x", "core")
    )
    return jax.shard_map(
        on_device,
        mesh=fine,
        in_specs=(
            P(BATCH, PROTO),
            P(None, PROTO + BATCH),
            P(BATCH, None),
            P(),
            P(BATCH, PROTO),
            P(BATCH),
            P(BATCH),
        ),
        out_specs=(P(BATCH, None), P(BATCH, PROTO)),
        check_vma=False,
    )
```

```python
import functools

import jax
import jax.numpy as jnp
from jax import lax
from jax.experimental import pallas as pl
from jax.experimental.pallas import tpu as pltpu
from jax.sharding import Mesh, PartitionSpec as P

ITERS = 3

teacher_scale = 3.0
student_scale = 2.0

BATCH = ("x", "core")
PROTO = ("z", "y")


def spread(block, axes):
    count = lax.axis_size(axes)
    return lax.all_to_all(
        jnp.broadcast_to(block[None], (count,) + block.shape),
        axes,
        split_axis=0,
        concat_axis=0,
        tiled=True,
    )


def exchange(parts, axes):
    return lax.all_to_all(parts, axes, split_axis=0, concat_axis=0, tiled=True)


def dot0(left, right):
    return lax.dot_general(
        left, right, (((0,), (0,)), ((), ())), preferred_element_type=jnp.float32
    )


def dot1(left, right):
    return lax.dot_general(
        left, right, (((1,), (1,)), ((), ())), preferred_element_type=jnp.float32
    )


def unfold_kernel(folded_ref, rows_ref):
    pairs, deep = folded_ref.shape[0] // 2, folded_ref.shape[1]
    lanes = folded_ref.shape[2]
    left = lax.broadcasted_iota(jnp.int32, (deep, lanes), 1) < lanes // 2
    for pair in range(pairs):
        even = folded_ref[2 * pair].astype(jnp.float32)
        odd = folded_ref[2 * pair + 1].astype(jnp.float32)
        upper = jnp.where(left, even, pltpu.roll(odd, lanes // 2, 1))
        lower = jnp.where(left, pltpu.roll(even, lanes // 2, 1), odd)
        columns = pl.ds(pair * lanes, lanes)
        rows_ref[0, 0:deep, columns] = upper.astype(jnp.bfloat16)
        rows_ref[0, deep : 2 * deep, columns] = lower.astype(jnp.bfloat16)


def unfold(folded, copies):
    count, deep, lanes = folded.shape
    width = count * lanes // 2
    return pl.pallas_call(
        unfold_kernel,
        grid=(copies,),
        in_specs=[pl.BlockSpec((count, deep, lanes), lambda i: (0, 0, 0))],
        out_specs=pl.BlockSpec((1, 2 * deep, width), lambda i: (i, 0, 0)),
        out_shape=jax.ShapeDtypeStruct((copies, 2 * deep, width), folded.dtype),
        compiler_params=pltpu.CompilerParams(vmem_limit_bytes=16 * 2**20),
        cost_estimate=pl.CostEstimate(
            flops=0, bytes_accessed=(copies + 1) * folded.size * 2, transcendentals=0
        ),
    )(folded)


def on_device(
    teacher_feats, teacher_protos, student_feats, crop_table, student_protos, assign, crop_ids
):
    core = lax.axis_index("core")
    n_proto, n_batch = lax.axis_size(PROTO), lax.axis_size(BATCH)
    images, features = teacher_feats.shape
    crops, width = student_feats.shape
    cols = teacher_protos.shape[1]
    swap = [(0, 1), (1, 0)]

    deep = images // 2
    rows = jnp.concatenate([teacher_feats[:deep], teacher_feats[deep:]], axis=1)
    their_protos = lax.ppermute(teacher_protos, "core", swap)
    rows = spread(rows, PROTO)
    rows, their_protos = lax.optimization_barrier((rows, their_protos))
    rows = exchange(unfold(rows, lax.axis_size("x")), "x")
    rows, student_protos = lax.optimization_barrier((rows, student_protos))
    full_protos = lax.all_gather(student_protos, BATCH, axis=0, tiled=True)

    contract = functools.partial(
        jnp.einsum, "xrk,kn->xrn", preferred_element_type=jnp.float32
    )
    theirs = contract(rows, their_protos)
    own = contract(rows, teacher_protos)
    got = lax.ppermute(theirs, "core", swap)
    first = core == 0
    products = jnp.stack([jnp.where(first, own, got), jnp.where(first, got, own)], axis=1)
    products = products.reshape(-1, cols)

    picks = (
        assign[:, None] == jnp.arange(images, dtype=jnp.int32)[None, :]
    ).astype(jnp.bfloat16)
    logits = teacher_scale * products
    weights = jnp.exp(logits - jnp.max(logits, axis=0, keepdims=True))
    for sweep in range(ITERS - 1):
        weights = lax.optimization_barrier(
            weights / jnp.sum(weights, axis=0, keepdims=True)
        )
        near = jnp.sum(spread(jnp.sum(weights, axis=1), ("z", "core")), axis=0)
        row_total = jnp.sum(spread(near, ("y", "x")), axis=0)
        if sweep == ITERS - 2:
            row_total, full_protos, student_feats, crop_table = lax.optimization_barrier(
                (row_total, full_protos, student_feats, crop_table)
            )
        weights = weights / row_total[:, None]
    weights = weights / jnp.sum(weights, axis=0, keepdims=True)

    chosen = (
        crop_ids[:, None] == jnp.arange(crop_table.shape[0], dtype=jnp.int32)[None, :]
    ).astype(jnp.bfloat16)
    table_rows = jnp.dot(chosen, crop_table, preferred_element_type=jnp.float32)
    hidden = (student_feats.astype(jnp.float32) + table_rows).astype(jnp.bfloat16)
    scores = student_scale * jnp.dot(hidden, full_protos, preferred_element_type=jnp.float32)
    peak = jnp.max(scores, axis=1)
    powers = jnp.exp(scores - peak[:, None])
    power_sum = jnp.sum(powers, axis=1)
    peak, powers, power_sum = lax.optimization_barrier((peak, powers, power_sum))

    mine = exchange(
        weights.astype(jnp.bfloat16).reshape(n_batch, images, cols), BATCH
    )
    mine = mine.transpose(1, 0, 2).reshape(images, -1)
    partial = jnp.sum(mine.astype(jnp.float32), axis=1)
    seen = spread(jnp.concatenate([partial, peak, power_sum]), PROTO)
    row_total = jnp.sum(seen[:, :images], axis=0)
    peaks, sums = seen[:, images : images + crops], seen[:, images + crops :]
    top = jnp.max(peaks, axis=0)
    denominator = jnp.sum(sums * jnp.exp(peaks - top[None]), axis=0)
    share = jnp.exp(peak - top) / denominator

    targets = (mine.astype(jnp.float32) / row_total[:, None]).astype(jnp.bfloat16)
    crop_targets = jnp.dot(picks, targets, preferred_element_type=jnp.float32)
    logit_grad = student_scale * (powers * share[:, None] - crop_targets)
    logit_grad = logit_grad.astype(jnp.bfloat16)

    feat_part = dot1(logit_grad, full_protos).astype(jnp.bfloat16)
    feat_part, logit_grad = lax.optimization_barrier((feat_part, logit_grad))
    feat_rows = feat_part.reshape(n_proto // 2, -1, 2, width // 2).transpose(0, 2, 1, 3)
    feat_rows = exchange(feat_rows.reshape(n_proto, -1, width // 2), PROTO)
    feat_rows = jnp.sum(feat_rows.astype(jnp.float32), axis=0).astype(jnp.bfloat16)
    feat_grad = spread(feat_rows, PROTO).reshape(n_proto // 2, 2, -1, width // 2)
    feat_grad = feat_grad.transpose(0, 2, 1, 3).reshape(crops, width)

    weight_grad = lax.psum_scatter(
        dot0(hidden, logit_grad).astype(jnp.bfloat16), BATCH, scatter_dimension=0, tiled=True
    )
    return (feat_grad, weight_grad)


def solution(mesh):
    n_proto, n_batch = mesh.shape["proto"], mesh.shape["batch"]
    side = 1
    while side * side < n_proto:
        side *= 2
    fine = Mesh(
        mesh.devices.reshape(n_proto // side, side, n_batch // 2, 2), ("z", "y", "x", "core")
    )
    return jax.shard_map(
        on_device,
        mesh=fine,
        in_specs=(
            P(BATCH, PROTO),
            P(None, PROTO + BATCH),
            P(BATCH, None),
            P(),
            P(BATCH, PROTO),
            P(BATCH),
            P(BATCH),
        ),
        out_specs=(P(BATCH, None), P(BATCH, PROTO)),
        check_vma=False,
    )
```
